256 devices in a mesh: sec: 8 (over z_hi, core), tp: 32 (over y, z_lo, x).
Axes of the slice: x: 4, y: 4, z: 8 (z_hi: 4, z_lo: 2; z = z_hi * 2 + z_lo), core: 2. Of those that a mesh axis runs over, the one named last changes fastest.
Arguments:
- down_act: bfloat16 [8, 256, 4096], P('sec', 'tp'), may hold values from -6 to 6
- down_stash: bfloat16 [8, 256, 4096], P('sec', 'tp'), may hold values from -6 to 6
- down_grad: bfloat16 [8, 256, 4096], P('sec', 'tp'), may hold values from -6 to 6
- up_act: bfloat16 [8, 256, 4096], P('sec', 'tp'), may hold values from -6 to 6
- up_stash: bfloat16 [8, 256, 4096], P('sec', 'tp'), may hold values from -6 to 6
- up_grad: bfloat16 [8, 256, 4096], P('sec', 'tp'), may hold values from -6 to 6
- w_in: bfloat16 [8, 4096, 12288], P('sec', None, 'tp'), may hold values from -0.09375 to 0.09375
- w_out: bfloat16 [8, 12288, 4096], P('sec', 'tp'), may hold values from -0.0546875 to 0.0546875
- norm_gain: float32 [8, 4096], P('sec'), may hold values from 0.5 to 1.5
Outputs:
- down_next: bfloat16 [8, 256, 4096], P('sec', 'tp')
- down_back: bfloat16 [8, 256, 4096], P('sec', 'tp')
- up_next: bfloat16 [8, 256, 4096], P('sec', 'tp')
- up_back: bfloat16 [8, 256, 4096], P('sec', 'tp')
- grad_in: bfloat16 [8, 4096, 12288], P('sec', None, 'tp')
- grad_out: bfloat16 [8, 12288, 4096], P('sec', 'tp')
- grad_gain: float32 [8, 4096], P('sec')
The draws below stay inside these ranges and needn't reach their ends.
All inputs are finite; a program needn't handle non-finite values.
Results may differ from the reference program's by a relative error of at most 0.0062.
Values may be sent and summed in bfloat16 or wider, within the bound.
No kernel may reach another device: no remote copies, remote signals or barrier semaphores. Data moves between devices by JAX's collectives and lax.ppermute only.
A program may use at most 128 MiB of HBM per device.

```python
import jax
import jax.numpy as jnp
from jax import lax

D = 4096
FF = 12288
TOK = 256
DEPTH = 8


def shard_levels(stream_key, shape, split, low, high):
    loudness = 1.0
    for axis_at, parts in split:
        draws = jax.random.uniform(jax.random.fold_in(jax.random.fold_in(stream_key, 6), axis_at), (parts,), jnp.float32, low / len(split), high / len(split))
        loudness = loudness * jnp.repeat(jnp.exp(draws), shape[axis_at] // parts).reshape((-1,) + (1,) * (len(shape) - 1 - axis_at))
    return loudness


def gaussian(key, shape, width, limit, pieces=(), held_as=jnp.bfloat16):
    array = width * jax.random.normal(key, shape, jnp.float32)
    if pieces:
        array = array * shard_levels(key, shape, pieces, -0.22, 0.18)
    return jnp.clip(array, -limit, limit).astype(held_as)


def setup_inputs(seed: int = 0) -> dict:
    splits = jax.random.split(jax.random.key(seed), 10)
    down_act = gaussian(splits[0], (DEPTH, TOK, D), 1.0, 6.0, ((0, 8), (1, 32)))
    down_stash = gaussian(splits[1], (DEPTH, TOK, D), 1.0, 6.0, ((0, 8), (1, 32)))
    down_grad = gaussian(splits[2], (DEPTH, TOK, D), 1.0, 6.0, ((0, 8), (1, 32)))
    up_act = gaussian(splits[3], (DEPTH, TOK, D), 1.0, 6.0, ((0, 8), (1, 32)))
    up_stash = gaussian(splits[4], (DEPTH, TOK, D), 1.0, 6.0, ((0, 8), (1, 32)))
    up_grad = gaussian(splits[5], (DEPTH, TOK, D), 1.0, 6.0, ((0, 8), (1, 32)))
    w_in = gaussian(splits[6], (DEPTH, D, FF), D ** -0.5, 0.09375, ((0, 8), (2, 32)))
    w_out = gaussian(splits[7], (DEPTH, FF, D), FF ** -0.5, 0.0546875, ((0, 8), (1, 32)))
    norm_gain = jnp.clip(1.0 + 0.1 * jax.random.normal(splits[8], (DEPTH, D), jnp.float32), 0.5, 1.5)
    return dict(down_act=down_act, down_stash=down_stash, down_grad=down_grad, up_act=up_act, up_stash=up_stash, up_grad=up_grad, w_in=w_in, w_out=w_out, norm_gain=norm_gain)


epsilon = 1e-05
root_coef = 0.7978845608028654
cubic_coef = 0.044715

def gelu_value(preact):
    inner = root_coef * (preact + cubic_coef * preact * preact * preact)
    return 0.5 * preact * (1.0 + jnp.tanh(inner))

def gelu_slope(preact):
    tanh_val = jnp.tanh(root_coef * (preact + cubic_coef * preact * preact * preact))
    return 0.5 * (1.0 + tanh_val) + 0.5 * preact * (1.0 - tanh_val * tanh_val) * root_coef * (1.0 + 3.0 * cubic_coef * preact * preact)

def normalize(activ, gain_row):
    widened = activ.astype(jnp.float32)
    row_scale = lax.rsqrt(lax.optimization_barrier(jnp.mean(widened * widened, axis=-1, keepdims=True)) + epsilon)
    return ((widened * row_scale * gain_row).astype(jnp.bfloat16), row_scale)

def forward_layer(activ, weight_in, weight_out, gain_row):
    normed, row_scale = normalize(activ, gain_row)
    preact = jnp.dot(normed, weight_in, preferred_element_type=jnp.float32)
    hidden = gelu_value(preact).astype(jnp.bfloat16)
    summed = jnp.dot(hidden, weight_out, preferred_element_type=jnp.float32)
    return (activ.astype(jnp.float32) + summed).astype(jnp.bfloat16)

def backward_layer(stash, cotangent, weight_in, weight_out, gain_row):
    widened = stash.astype(jnp.float32)
    normed, row_scale = normalize(stash, gain_row)
    preact = jnp.dot(normed, weight_in, preferred_element_type=jnp.float32)
    hidden = gelu_value(preact).astype(jnp.bfloat16)
    grad_out_part = jnp.dot(hidden.T, cotangent, preferred_element_type=jnp.float32)
    slope_grad = (jnp.dot(cotangent, weight_out.T, preferred_element_type=jnp.float32) * gelu_slope(preact)).astype(jnp.bfloat16)
    grad_in_part = jnp.dot(normed.T, slope_grad, preferred_element_type=jnp.float32)
    dnorm = jnp.dot(slope_grad, weight_in.T, preferred_element_type=jnp.float32)
    weighted = dnorm * gain_row
    mixed_term = lax.optimization_barrier(jnp.mean(weighted * widened, axis=-1, keepdims=True))
    input_grad = cotangent.astype(jnp.float32) + row_scale * weighted - widened * row_scale * row_scale * row_scale * mixed_term
    gain_part = lax.optimization_barrier(jnp.sum(dnorm * widened * row_scale, axis=0))
    return (input_grad.astype(jnp.bfloat16), grad_in_part, grad_out_part, gain_part)

def reference(down_act, down_stash, down_grad, up_act, up_stash, up_grad, w_in, w_out, norm_gain):

    def per_layer(layer):
        mirror = DEPTH - 1 - layer
        weight_in = w_in[layer]
        weight_out = w_out[layer]
        gain_row = norm_gain[layer]
        next_down = forward_layer(down_act[layer], weight_in, weight_out, gain_row)
        back_down, in_down, out_down, gain_down = backward_layer(down_stash[layer], down_grad[layer], weight_in, weight_out, gain_row)
        next_up = forward_layer(up_act[mirror], weight_in, weight_out, gain_row)
        back_up, in_up, out_up, gain_up = backward_layer(up_stash[mirror], up_grad[mirror], weight_in, weight_out, gain_row)
        return (next_down, back_down, next_up, back_up, (in_down + in_up).astype(jnp.bfloat16), (out_down + out_up).astype(jnp.bfloat16), gain_down + gain_up)
    layers = jnp.arange(DEPTH, dtype=jnp.int32)
    next_down, back_down, next_up, back_up, grad_in, grad_out, grad_gain = lax.map(per_layer, layers)
    blank = jnp.zeros((1, TOK, D), jnp.bfloat16)
    down_next = jnp.concatenate([blank, next_down[:-1]], axis=0)
    down_back = jnp.concatenate([back_down[1:], blank], axis=0)
    up_next = jnp.concatenate([jnp.flip(next_up, 0)[1:], blank], axis=0)
    up_back = jnp.concatenate([blank, jnp.flip(back_up, 0)[:-1]], axis=0)
    return (down_next, down_back, up_next, up_back, grad_in, grad_out, grad_gain)
```

```python
import jax
import jax.numpy as jnp
from jax import lax
from jax.sharding import Mesh
from jax.sharding import PartitionSpec as P

epsilon = 1e-05
root_coef = 0.7978845608028654
cubic_coef = 0.044715

f32 = jnp.float32
bf16 = jnp.bfloat16

AXES = ("zh", "core", "y", "zl", "x")
SIZES = {"x": 4, "y": 4, "zl": 2}
SEC = ("zh", "core")
TP = ("y", "zl", "x")


def shift(value, axis, k):
    n = SIZES[axis]
    return lax.ppermute(value, axis, [(i, (i + k) % n) for i in range(n)])


def gelu_both(preact):
    tanh_val = jnp.tanh(root_coef * (preact + cubic_coef * preact * preact * preact))
    value = 0.5 * preact * (1.0 + tanh_val)
    slope = 0.5 * (1.0 + tanh_val) + 0.5 * preact * (1.0 - tanh_val * tanh_val) * root_coef * (
        1.0 + 3.0 * cubic_coef * preact * preact
    )
    return value, slope


def row_scale_of(activ):
    widened = activ.astype(f32)
    return lax.rsqrt(jnp.mean(widened * widened, axis=-1, keepdims=True) + epsilon)


def contract_last(left, right):
    return lax.dot_general(left, right, (((1,), (1,)), ((), ())), preferred_element_type=f32)


def contract_first(left, right):
    return lax.dot_general(left, right, (((0,), (0,)), ((), ())), preferred_element_type=f32)


def gather_starts(block, axis):
    return [block] + [shift(block, axis, -k) for k in range(1, SIZES[axis])]


def lockstep(groups):
    return lax.optimization_barrier(groups)


GATHER = (("zl", "y", "x"), ("x", "zl", "y"), ("y", "x", "zl"))
SCATTER = (("x", "y", "zl"), ("y", "zl", "x"), ("zl", "x", "y"))


def gather_all(blocks):
    current = list(blocks)
    for stage in range(3):
        pieces = [gather_starts(c, GATHER[i][stage]) for i, c in enumerate(current)]
        pieces = lockstep(pieces)
        current = [jnp.stack(p, axis=1) for p in pieces]
        current = [c.reshape((c.shape[0], c.shape[1] * c.shape[2]) + c.shape[3:]) for c in current]
    return current


def to_common(array, order):
    kinds, _, width = array.shape
    sizes = [SIZES[a] for a in reversed(order)]
    v = array.reshape([kinds] + sizes + [8, width])
    names = list(reversed(order))
    perm = [0] + [1 + names.index(a) for a in ("x", "y", "zl")] + [4, 5]
    return v.transpose(perm)


def scatter_stage(part, axis, names):
    at = 1 + names.index(axis)
    own = lax.index_in_dim(part, 0, at, keepdims=False)
    got = [
        shift(lax.index_in_dim(part, k, at, keepdims=False).astype(bf16), axis, k)
        for k in range(1, SIZES[axis])
    ]
    return own, got


def scatter_all(parts):
    current = list(parts)
    names = [["x", "y", "zl"] for _ in parts]
    for stage in range(3):
        moved = []
        for i, c in enumerate(current):
            axis = SCATTER[i][stage]
            moved.append(scatter_stage(c, axis, names[i]))
            names[i].remove(axis)
        moved = lockstep(moved)
        current = [own.astype(f32) + sum(g.astype(f32) for g in got) for own, got in moved]
    return current


SPLITS = (0, 1536, 3072, 4096)


def body(down_act, down_stash, down_grad, up_act, up_stash, up_grad, w_in, w_out, norm_gain):
    weight_in = w_in[0]
    weight_out = w_out[0]
    gain_row = norm_gain[0]
    segments = 8
    mirror = [(i, segments - 1 - i) for i in range(segments)]
    incoming = jnp.stack([up_act[0], up_stash[0], up_grad[0]])
    far = lax.ppermute(incoming, SEC, mirror)
    act = jnp.stack([down_act[0], far[0]])
    stash = jnp.stack([down_stash[0], far[1]])
    grad = jnp.stack([down_grad[0], far[2]])
    stash_scale = row_scale_of(stash)

    act_normed = (act.astype(f32) * row_scale_of(act) * gain_row).astype(bf16)
    stash_normed = (stash.astype(f32) * stash_scale * gain_row).astype(bf16)

    back_down, back_up, ahead = gather_all(
        [
            jnp.stack([stash_normed[0], grad[0]]),
            jnp.stack([stash_normed[1], grad[1]]),
            act_normed,
        ]
    )
    width = ahead.shape[-1]
    ahead = to_common(ahead, GATHER[2]).reshape(-1, width)
    back_down = to_common(back_down, GATHER[0]).reshape(2, -1, width)
    back_up = to_common(back_up, GATHER[1]).reshape(2, -1, width)
    normed = jnp.concatenate([back_down[0], back_up[0]])
    cot = jnp.concatenate([back_down[1], back_up[1]])

    hidden_ahead, _ = gelu_both(jnp.dot(ahead, weight_in, preferred_element_type=f32))
    hidden_ahead = hidden_ahead.astype(bf16)
    summed_part = jnp.dot(hidden_ahead, weight_out, preferred_element_type=f32).astype(bf16)
    value, slope = gelu_both(jnp.dot(normed, weight_in, preferred_element_type=f32))
    hidden = value.astype(bf16)
    slope_grad = (contract_last(cot, weight_out) * slope).astype(bf16)
    dnorm_part = contract_last(slope_grad, weight_in).astype(bf16)

    parts = jnp.concatenate([summed_part, dnorm_part]).reshape(4, 4, 4, 2, 8, width)
    totals = scatter_all(
        [parts[..., SPLITS[i] : SPLITS[i + 1]] for i in range(3)]
    )
    total = jnp.concatenate(totals, axis=-1)

    grad_out = contract_first(hidden, cot).astype(bf16)
    grad_in_wide = contract_first(normed, slope_grad)
    grad_in = grad_in_wide.astype(bf16)
    gain_sum = jnp.sum(grad_in_wide * weight_in.astype(f32), axis=1) / gain_row
    for axis, bit in (("x", 1), ("x", 2), ("y", 1), ("y", 2), ("zl", 1)):
        gain_sum = gain_sum + lax.ppermute(
            gain_sum, axis, [(i, i ^ bit) for i in range(SIZES[axis])]
        )

    nexts = (act.astype(f32) + total[:2]).astype(bf16)
    widened = stash.astype(f32)
    weighted = total[2:] * gain_row
    mixed_term = jnp.mean(weighted * widened, axis=-1, keepdims=True)
    backs = (
        grad.astype(f32)
        + stash_scale * weighted
        - widened * stash_scale * stash_scale * stash_scale * mixed_term
    ).astype(bf16)

    down_next = lax.ppermute(nexts[0], SEC, [(i, i + 1) for i in range(segments - 1)])
    down_back = lax.ppermute(backs[0], SEC, [(i, i - 1) for i in range(1, segments)])
    up_next = lax.ppermute(nexts[1], SEC, [(i, segments - 2 - i) for i in range(segments - 1)])
    up_back = lax.ppermute(backs[1], SEC, [(i, segments - i) for i in range(1, segments)])
    return (
        down_next[None],
        down_back[None],
        up_next[None],
        up_back[None],
        grad_in[None],
        grad_out[None],
        gain_sum[None],
    )


def solution(mesh):
    fine = Mesh(mesh.devices.reshape(4, 2, 4, 2, 4), AXES)
    tokens = P(SEC, TP, None)
    return jax.shard_map(
        body,
        mesh=fine,
        in_specs=(tokens,) * 6 + (P(SEC, None, TP), P(SEC, TP, None), P(SEC, None)),
        out_specs=(tokens,) * 4 + (P(SEC, None, TP), P(SEC, TP, None), P(SEC, None)),
        check_vma=False,
    )
```

```python
import jax
import jax.numpy as jnp
from jax import lax
from jax.sharding import Mesh
from jax.sharding import PartitionSpec as P

epsilon = 1e-05
root_coef = 0.7978845608028654
cubic_coef = 0.044715

f32 = jnp.float32
bf16 = jnp.bfloat16

AXES = ("zh", "core", "y", "zl", "x")
SIZES = {"x": 4, "y": 4, "zl": 2}
SEC = ("zh", "core")
TP = ("y", "zl", "x")


def shift(value, axis, k):
    n = SIZES[axis]
    return lax.ppermute(value, axis, [(i, (i + k) % n) for i in range(n)])


def gelu_both(preact):
    tanh_val = jnp.tanh(root_coef * (preact + cubic_coef * preact * preact * preact))
    value = 0.5 * preact * (1.0 + tanh_val)
    slope = 0.5 * (1.0 + tanh_val) + 0.5 * preact * (1.0 - tanh_val * tanh_val) * root_coef * (
        1.0 + 3.0 * cubic_coef * preact * preact
    )
    return value, slope


def row_scale_of(activ):
    widened = activ.astype(f32)
    return lax.rsqrt(jnp.mean(widened * widened, axis=-1, keepdims=True) + epsilon)


def contract_last(left, right):
    return lax.dot_general(left, right, (((1,), (1,)), ((), ())), preferred_element_type=f32)


def contract_first(left, right):
    return lax.dot_general(left, right, (((0,), (0,)), ((), ())), preferred_element_type=f32)


def gather_stage(block, axis):
    if SIZES[axis] == 2:
        return jnp.concatenate([block, shift(block, axis, 1)], axis=1)
    half = block.shape[1] // 2
    ahead = shift(block, axis, -1)
    behind = shift(block, axis, 1)
    far_low = shift(ahead[:, :half], axis, -1)
    far_high = shift(behind[:, half:], axis, 1)
    return jnp.concatenate([block, ahead, far_low, far_high, behind], axis=1)


def gather(block, order):
    for axis in order:
        block = gather_stage(block, axis)
    return block


def scatter_stage(part, axis):
    n = SIZES[axis]
    m = part.shape[1] // n
    half = m // 2
    own = part[:, :m].astype(f32)
    if n == 2:
        return own + shift(part[:, m:], axis, 1).astype(f32)
    relay_low = shift(part[:, 2 * m : 2 * m + half], axis, 1)
    relay_high = shift(part[:, 2 * m + half : 3 * m], axis, -1)
    to_next = part[:, m : 2 * m]
    to_last = part[:, 3 * m :]
    to_next = jnp.concatenate(
        [(to_next[:, :half].astype(f32) + relay_low.astype(f32)).astype(bf16), to_next[:, half:]], axis=1
    )
    to_last = jnp.concatenate(
        [to_last[:, :half], (to_last[:, half:].astype(f32) + relay_high.astype(f32)).astype(bf16)], axis=1
    )
    return own + shift(to_next, axis, 1).astype(f32) + shift(to_last, axis, -1).astype(f32)


def scatter(part, order):
    for axis in order[:-1]:
        part = scatter_stage(part, axis).astype(bf16)
    return scatter_stage(part, order[-1])


def work(act_normed, stash_normed, cot, weight_in, weight_out):
    tokens = act_normed.shape[0]
    hidden_ahead, _ = gelu_both(jnp.dot(act_normed, weight_in, preferred_element_type=f32))
    summed = jnp.dot(hidden_ahead.astype(bf16), weight_out, preferred_element_type=f32).astype(bf16)
    value, slope = gelu_both(jnp.dot(stash_normed, weight_in, preferred_element_type=f32))
    slope_grad = (contract_last(cot, weight_out) * slope).astype(bf16)
    dnorm = contract_last(slope_grad, weight_in).astype(bf16)
    return jnp.stack([summed, dnorm]), value.astype(bf16), slope_grad


def finish(act, stash, grad, scale, total, gain_row):
    ahead = (act.astype(f32) + total[0]).astype(bf16)
    widened = stash.astype(f32)
    weighted = total[1] * gain_row
    mixed_term = jnp.mean(weighted * widened, axis=-1, keepdims=True)
    back = (
        grad.astype(f32) + scale * weighted - widened * scale * scale * scale * mixed_term
    ).astype(bf16)
    return ahead, back


def prepare(act, stash, grad, gain_row):
    scale = row_scale_of(stash)
    act_normed = (act.astype(f32) * row_scale_of(act) * gain_row).astype(bf16)
    stash_normed = (stash.astype(f32) * scale * gain_row).astype(bf16)
    return jnp.stack([act_normed, stash_normed, grad]), scale


def body(down_act, down_stash, down_grad, up_act, up_stash, up_grad, w_in, w_out, norm_gain):
    weight_in = w_in[0]
    weight_out = w_out[0]
    gain_row = norm_gain[0]
    segments = 8
    mirror = [(i, segments - 1 - i) for i in range(segments)]
    incoming = jnp.stack([up_act[0], up_stash[0], up_grad[0]])
    far = lax.ppermute(incoming, SEC, mirror)
    near_block, near_scale = prepare(down_act[0], down_stash[0], down_grad[0], gain_row)
    far_block, far_scale = prepare(far[0], far[1], far[2], gain_row)
    near_full = gather(near_block, ("zl", "y", "x"))
    far_full = gather(far_block, ("zl", "x", "y"))

    near_part, near_hidden, near_slope = work(
        near_full[0], near_full[1], near_full[2], weight_in, weight_out
    )
    far_part, far_hidden, far_slope = work(
        far_full[0], far_full[1], far_full[2], weight_in, weight_out
    )
    near_total = scatter(near_part, ("x", "y", "zl"))
    far_total = scatter(far_part, ("y", "x", "zl"))

    normed = jnp.concatenate([near_full[1], far_full[1]])
    cot = jnp.concatenate([near_full[2], far_full[2]])
    hidden = jnp.concatenate([near_hidden, far_hidden])
    slope_grad = jnp.concatenate([near_slope, far_slope])
    grad_out = contract_first(hidden, cot).astype(bf16)
    grad_in_wide = contract_first(normed, slope_grad)
    grad_in = grad_in_wide.astype(bf16)
    gain_sum = jnp.sum(grad_in_wide * weight_in.astype(f32), axis=1) / gain_row
    for axis, bit in (("x", 1), ("x", 2), ("y", 1), ("y", 2), ("zl", 1)):
        gain_sum = gain_sum + lax.ppermute(
            gain_sum, axis, [(i, i ^ bit) for i in range(SIZES[axis])]
        )

    next_down, back_down = finish(
        down_act[0], down_stash[0], down_grad[0], near_scale, near_total, gain_row
    )
    next_up, back_up = finish(far[0], far[1], far[2], far_scale, far_total, gain_row)

    down_next = lax.ppermute(next_down, SEC, [(i, i + 1) for i in range(segments - 1)])
    down_back = lax.ppermute(back_down, SEC, [(i, i - 1) for i in range(1, segments)])
    up_next = lax.ppermute(next_up, SEC, [(i, segments - 2 - i) for i in range(segments - 1)])
    up_back = lax.ppermute(back_up, SEC, [(i, segments - i) for i in range(1, segments)])
    return (
        down_next[None],
        down_back[None],
        up_next[None],
        up_back[None],
        grad_in[None],
        grad_out[None],
        gain_sum[None],
    )


def solution(mesh):
    fine = Mesh(mesh.devices.reshape(4, 2, 4, 2, 4), AXES)
    tokens = P(SEC, TP, None)
    return jax.shard_map(
        body,
        mesh=fine,
        in_specs=(tokens,) * 6 + (P(SEC, None, TP), P(SEC, TP, None), P(SEC, None)),
        out_specs=(tokens,) * 4 + (P(SEC, None, TP), P(SEC, TP, None), P(SEC, None)),
        check_vma=False,
    )
```

```python
import jax
import jax.numpy as jnp
from jax import lax
from jax.sharding import Mesh
from jax.sharding import PartitionSpec as P

epsilon = 1e-05
root_coef = 0.7978845608028654
cubic_coef = 0.044715

f32 = jnp.float32
bf16 = jnp.bfloat16

AXES = ("zh", "core", "y", "zl", "x")
SIZES = {"x": 4, "y": 4, "zl": 2}
SEC = ("zh", "core")
TP = ("y", "zl", "x")


def shift(value, axis, k):
    n = SIZES[axis]
    return lax.ppermute(value, axis, [(i, (i + k) % n) for i in range(n)])


def gelu_both(preact):
    tanh_val = jnp.tanh(root_coef * (preact + cubic_coef * preact * preact * preact))
    value = 0.5 * preact * (1.0 + tanh_val)
    slope = 0.5 * (1.0 + tanh_val) + 0.5 * preact * (1.0 - tanh_val * tanh_val) * root_coef * (
        1.0 + 3.0 * cubic_coef * preact * preact
    )
    return value, slope


def row_scale_of(activ):
    widened = activ.astype(f32)
    return lax.rsqrt(jnp.mean(widened * widened, axis=-1, keepdims=True) + epsilon)


def contract_last(left, right):
    return lax.dot_general(left, right, (((1,), (1,)), ((), ())), preferred_element_type=f32)


def contract_first(left, right):
    return lax.dot_general(left, right, (((0,), (0,)), ((), ())), preferred_element_type=f32)


def scatter_direct(part, axis):
    m = part.shape[1] // SIZES[axis]
    total = part[:, :m].astype(f32)
    for k in range(1, SIZES[axis]):
        total = total + shift(part[:, k * m : (k + 1) * m], axis, k).astype(f32)
    return total


def added(left, right):
    return (left.astype(f32) + right.astype(f32)).astype(bf16)


def ring(block, axis):
    return shift(block, axis, -1), shift(block, axis, 1)


def ring_far(ahead, behind, axis):
    half = ahead.shape[1] // 2
    return shift(ahead[:, :half], axis, -1), shift(behind[:, half:], axis, 1)


def send_far(part, axis):
    m = part.shape[1] // 4
    half = m // 2
    far = part[:, 2 * m : 3 * m]
    return shift(far[:, :half], axis, 1), shift(far[:, half:], axis, -1)


def hand_over(part, low, high, axis):
    m = part.shape[1] // 4
    half = m // 2
    to_next = jnp.concatenate([added(part[:, m : m + half], low), part[:, m + half : 2 * m]], axis=1)
    to_last = jnp.concatenate([part[:, 3 * m : 3 * m + half], added(part[:, 3 * m + half :], high)], axis=1)
    return shift(to_next, axis, 1), shift(to_last, axis, -1)


def own_sum(part, from_last, from_next):
    m = part.shape[1] // 4
    return (part[:, :m].astype(f32) + from_last.astype(f32) + from_next.astype(f32)).astype(bf16)


def joined(block, ahead, low, high, behind):
    return jnp.concatenate([block, ahead, low, high, behind], axis=1)


def exchange(value, axis, bit):
    return value + lax.ppermute(value, axis, [(i, i ^ bit) for i in range(SIZES[axis])])


barrier = lax.optimization_barrier


def finish(act, stash, grad, scale, total, gain_row):
    ahead = (act.astype(f32) + total[0]).astype(bf16)
    widened = stash.astype(f32)
    weighted = total[1] * gain_row
    mixed_term = jnp.mean(weighted * widened, axis=-1, keepdims=True)
    back = (
        grad.astype(f32) + scale * weighted - widened * scale * scale * scale * mixed_term
    ).astype(bf16)
    return ahead, back


def prepare(act, stash, grad, gain_row):
    scale = row_scale_of(stash)
    act_normed = (act.astype(f32) * row_scale_of(act) * gain_row).astype(bf16)
    stash_normed = (stash.astype(f32) * scale * gain_row).astype(bf16)
    return jnp.stack([act_normed, stash_normed, grad]), scale


def body(down_act, down_stash, down_grad, up_act, up_stash, up_grad, w_in, w_out, norm_gain):
    weight_in = w_in[0]
    weight_out = w_out[0]
    gain_row = norm_gain[0]
    segments = 8
    mirror = [(i, segments - 1 - i) for i in range(segments)]
    incoming = jnp.stack([up_act[0], up_stash[0], up_grad[0]])
    far = lax.ppermute(incoming, SEC, mirror)
    near_block, near_scale = prepare(down_act[0], down_stash[0], down_grad[0], gain_row)
    near = jnp.concatenate([near_block, shift(near_block, "zl", 1)], axis=1)
    far, far_gain = barrier((far, gain_row))
    far_block, far_scale = prepare(far[0], far[1], far[2], far_gain)
    away = jnp.concatenate([far_block, shift(far_block, "zl", 1)], axis=1)

    near, away = barrier((near, away))
    na, nb = ring(near, "y")
    fa, fb = ring(away, "x")
    near = joined(near, na, *ring_far(na, nb, "y"), nb)
    away = joined(away, fa, *ring_far(fa, fb, "x"), fb)
    near, away = barrier((near, away))
    na, nb = ring(near, "x")
    fa, fb = ring(away, "y")
    nl, nh = ring_far(na, nb, "x")
    fl, fh = ring_far(fa, fb, "y")
    pieces = (near, na, nl, nh, nb, away, fa, fl, fh, fb)
    acts, normed, cot = [jnp.concatenate([p[k] for p in pieces]) for k in range(3)]

    hidden_ahead, _ = gelu_both(jnp.dot(acts, weight_in, preferred_element_type=f32))
    summed = jnp.dot(hidden_ahead.astype(bf16), weight_out, preferred_element_type=f32).astype(bf16)
    value, slope = gelu_both(jnp.dot(normed, weight_in, preferred_element_type=f32))
    hidden = value.astype(bf16)
    slope_grad = (contract_last(cot, weight_out) * slope).astype(bf16)
    dnorm = contract_last(slope_grad, weight_in).astype(bf16)

    rows = acts.shape[0] // 2
    near_part = jnp.stack([summed[:rows], dnorm[:rows]])
    far_part = jnp.stack([summed[rows:], dnorm[rows:]])
    nl, nh = send_far(near_part, "x")
    fl, fh = send_far(far_part, "y")
    nl, nh, fl, fh, hidden, slope_grad = barrier((nl, nh, fl, fh, hidden, slope_grad))
    n1, n3 = hand_over(near_part, nl, nh, "x")
    f1, f3 = hand_over(far_part, fl, fh, "y")
    grad_in_wide = contract_first(normed, slope_grad)
    grad_in = grad_in_wide.astype(bf16)
    gain_sum = jnp.sum(grad_in_wide * weight_in.astype(f32), axis=1) / gain_row
    grad_out = contract_first(hidden, cot).astype(bf16)
    gain_sum = exchange(exchange(gain_sum, "x", 1), "x", 2)
    n1, n3, f1, f3, gain_sum = barrier((n1, n3, f1, f3, gain_sum))

    near_part, far_part = own_sum(near_part, n1, n3), own_sum(far_part, f1, f3)
    near_part = scatter_direct(near_part, "y").astype(bf16)
    far_part = scatter_direct(far_part, "x").astype(bf16)
    gain_sum = exchange(gain_sum, "y", 1)
    near_part, far_part, gain_sum, grad_out = barrier((near_part, far_part, gain_sum, grad_out))
    near_total = scatter_direct(near_part, "zl")
    far_total = scatter_direct(far_part, "zl")
    gain_sum = exchange(gain_sum, "y", 2)

    next_down, back_down = finish(
        down_act[0], down_stash[0], down_grad[0], near_scale, near_total, gain_row
    )
    next_up, back_up = finish(far[0], far[1], far[2], far_scale, far_total, gain_row)

    next_down, back_down, next_up, back_up, gain_sum = barrier(
        (next_down, back_down, next_up, back_up, gain_sum)
    )
    gain_sum = exchange(gain_sum, "zl", 1)
    down_next = lax.ppermute(next_down, SEC, [(i, i + 1) for i in range(segments - 1)])
    down_back = lax.ppermute(back_down, SEC, [(i, i - 1) for i in range(1, segments)])
    up_next = lax.ppermute(next_up, SEC, [(i, segments - 2 - i) for i in range(segments - 1)])
    up_back = lax.ppermute(back_up, SEC, [(i, segments - i) for i in range(1, segments)])
    return (
        down_next[None],
        down_back[None],
        up_next[None],
        up_back[None],
        grad_in[None],
        grad_out[None],
        gain_sum[None],
    )


def solution(mesh):
    fine = Mesh(mesh.devices.reshape(4, 2, 4, 2, 4), AXES)
    tokens = P(SEC, TP, None)
    return jax.shard_map(
        body,
        mesh=fine,
        in_specs=(tokens,) * 6 + (P(SEC, None, TP), P(SEC, TP, None), P(SEC, None)),
        out_specs=(tokens,) * 4 + (P(SEC, None, TP), P(SEC, TP, None), P(SEC, None)),
        check_vma=False,
    )
```

```python
import jax
import jax.numpy as jnp
from jax.experimental import pallas as pl
from jax.experimental.pallas import tpu as pltpu
from jax import lax
from jax.sharding import Mesh
from jax.sharding import PartitionSpec as P

epsilon = 1e-05
root_coef = 0.7978845608028654
cubic_coef = 0.044715

f32 = jnp.float32
bf16 = jnp.bfloat16

AXES = ("zh", "core", "y", "zl", "x")
SIZES = {"x": 4, "y": 4, "zl": 2}
SEC = ("zh", "core")
TP = ("y", "zl", "x")


def shift(value, axis, k):
    n = SIZES[axis]
    return lax.ppermute(value, axis, [(i, (i + k) % n) for i in range(n)])


def gelu_both(preact):
    tanh_val = jnp.tanh(root_coef * (preact + cubic_coef * preact * preact * preact))
    value = 0.5 * preact * (1.0 + tanh_val)
    slope = 0.5 * (1.0 + tanh_val) + 0.5 * preact * (1.0 - tanh_val * tanh_val) * root_coef * (
        1.0 + 3.0 * cubic_coef * preact * preact
    )
    return value, slope


def row_scale_of(activ):
    widened = activ.astype(f32)
    return lax.rsqrt(jnp.mean(widened * widened, axis=-1, keepdims=True) + epsilon)


def contract_last(left, right):
    return lax.dot_general(left, right, (((1,), (1,)), ((), ())), preferred_element_type=f32)


def contract_first(left, right):
    return lax.dot_general(left, right, (((0,), (0,)), ((), ())), preferred_element_type=f32)


def scatter_direct(part, axis):
    m = part.shape[1] // SIZES[axis]
    total = part[:, :m].astype(f32)
    for k in range(1, SIZES[axis]):
        total = total + shift(part[:, k * m : (k + 1) * m], axis, k).astype(f32)
    return total


def added(left, right):
    return (left.astype(f32) + right.astype(f32)).astype(bf16)


def ring(block, axis):
    return shift(block, axis, -1), shift(block, axis, 1)


def ring_far(ahead, behind, axis):
    half = ahead.shape[1] // 2
    return shift(ahead[:, :half], axis, -1), shift(behind[:, half:], axis, 1)


def send_far(part, axis):
    m = part.shape[1] // 4
    half = m // 2
    far = part[:, 2 * m : 3 * m]
    return shift(far[:, :half], axis, 1), shift(far[:, half:], axis, -1)


def hand_over(part, low, high, axis):
    m = part.shape[1] // 4
    half = m // 2
    to_next = jnp.concatenate([added(part[:, m : m + half], low), part[:, m + half : 2 * m]], axis=1)
    to_last = jnp.concatenate([part[:, 3 * m : 3 * m + half], added(part[:, 3 * m + half :], high)], axis=1)
    return shift(to_next, axis, 1), shift(to_last, axis, -1)


def own_sum(part, from_last, from_next):
    m = part.shape[1] // 4
    return (part[:, :m].astype(f32) + from_last.astype(f32) + from_next.astype(f32)).astype(bf16)


def joined(block, ahead, low, high, behind):
    return jnp.concatenate([block, ahead, low, high, behind], axis=1)


def exchange(value, axis, bit):
    return value + lax.ppermute(value, axis, [(i, i ^ bit) for i in range(SIZES[axis])])


def weight_grad_kernel(normed_ref, slope_ref, weight_ref, grad_ref, gain_ref):
    grad = contract_first(normed_ref[...], slope_ref[...])
    grad_ref[...] = grad.astype(bf16)
    ones = jnp.ones((8, grad.shape[1]), f32)
    gain_ref[...] = lax.dot_general(
        ones,
        grad * weight_ref[...].astype(f32),
        (((1,), (1,)), ((), ())),
        precision=lax.Precision.HIGHEST,
        preferred_element_type=f32,
    )


def weight_grad(normed, slope_grad, weight_in):
    tokens, width = normed.shape
    units = slope_grad.shape[1]
    tile = 512
    return pl.pallas_call(
        weight_grad_kernel,
        grid=(width // tile,),
        in_specs=[
            pl.BlockSpec((tokens, tile), lambda i: (0, i)),
            pl.BlockSpec((tokens, units), lambda i: (0, 0)),
            pl.BlockSpec((tile, units), lambda i: (i, 0)),
        ],
        out_specs=[
            pl.BlockSpec((tile, units), lambda i: (i, 0)),
            pl.BlockSpec((8, tile), lambda i: (0, i)),
        ],
        out_shape=[
            jax.ShapeDtypeStruct((width, units), bf16),
            jax.ShapeDtypeStruct((8, width), f32),
        ],
        compiler_params=pltpu.CompilerParams(vmem_limit_bytes=16 * 2**20),
        cost_estimate=pl.CostEstimate(
            flops=2 * tokens * width * units,
            bytes_accessed=2 * (tokens * width + 2 * width * units),
            transcendentals=0,
        ),
    )(normed, slope_grad, weight_in)


barrier = lax.optimization_barrier


def finish(act, stash, grad, scale, total, gain_row):
    ahead = (act.astype(f32) + total[0]).astype(bf16)
    widened = stash.astype(f32)
    weighted = total[1] * gain_row
    mixed_term = jnp.mean(weighted * widened, axis=-1, keepdims=True)
    back = (
        grad.astype(f32) + scale * weighted - widened * scale * scale * scale * mixed_term
    ).astype(bf16)
    return ahead, back


def prepare(act, stash, grad, gain_row):
    scale = row_scale_of(stash)
    act_normed = (act.astype(f32) * row_scale_of(act) * gain_row).astype(bf16)
    stash_normed = (stash.astype(f32) * scale * gain_row).astype(bf16)
    return jnp.stack([act_normed, stash_normed, grad]), scale


def body(down_act, down_stash, down_grad, up_act, up_stash, up_grad, w_in, w_out, norm_gain):
    weight_in = w_in[0]
    weight_out = w_out[0]
    gain_row = norm_gain[0]
    segments = 8
    mirror = [(i, segments - 1 - i) for i in range(segments)]
    incoming = jnp.stack([up_act[0], up_stash[0], up_grad[0]])
    far = lax.ppermute(incoming, SEC, mirror)
    near_block, near_scale = prepare(down_act[0], down_stash[0], down_grad[0], gain_row)
    near = jnp.concatenate([near_block, shift(near_block, "zl", 1)], axis=1)
    far, far_gain = barrier((far, gain_row))
    far_block, far_scale = prepare(far[0], far[1], far[2], far_gain)
    away = jnp.concatenate([far_block, shift(far_block, "zl", 1)], axis=1)

    near, away = barrier((near, away))
    na, nb = ring(near, "y")
    fa, fb = ring(away, "x")
    near = joined(near, na, *ring_far(na, nb, "y"), nb)
    away = joined(away, fa, *ring_far(fa, fb, "x"), fb)
    near, away = barrier((near, away))
    na, nb = ring(near, "x")
    fa, fb = ring(away, "y")
    nl, nh = ring_far(na, nb, "x")
    fl, fh = ring_far(fa, fb, "y")
    pieces = (near, na, nl, nh, nb, away, fa, fl, fh, fb)
    acts, normed, cot = [jnp.concatenate([p[k] for p in pieces]) for k in range(3)]

    hidden_ahead, _ = gelu_both(jnp.dot(acts, weight_in, preferred_element_type=f32))
    hidden_ahead = barrier(hidden_ahead.astype(bf16))
    summed = jnp.dot(hidden_ahead, weight_out, preferred_element_type=f32).astype(bf16)
    value, slope = gelu_both(jnp.dot(normed, weight_in, preferred_element_type=f32))
    hidden = value.astype(bf16)
    slope_grad = (contract_last(cot, weight_out) * slope).astype(bf16)
    dnorm = contract_last(slope_grad, weight_in).astype(bf16)

    rows = acts.shape[0] // 2
    near_part = jnp.stack([summed[:rows], dnorm[:rows]])
    far_part = jnp.stack([summed[rows:], dnorm[rows:]])
    nl, nh = send_far(near_part, "x")
    fl, fh = send_far(far_part, "y")
    nl, nh, fl, fh, hidden, slope_grad = barrier((nl, nh, fl, fh, hidden, slope_grad))
    n1, n3 = hand_over(near_part, nl, nh, "x")
    f1, f3 = hand_over(far_part, fl, fh, "y")
    grad_in, gain_rows = weight_grad(normed, slope_grad, weight_in)
    gain_sum = gain_rows[0] / gain_row
    grad_out = contract_first(hidden, cot).astype(bf16)
    gain_sum = exchange(exchange(gain_sum, "x", 1), "x", 2)
    n1, n3, f1, f3, gain_sum = barrier((n1, n3, f1, f3, gain_sum))

    near_part, far_part = own_sum(near_part, n1, n3), own_sum(far_part, f1, f3)
    near_part = scatter_direct(near_part, "y").astype(bf16)
    far_part = scatter_direct(far_part, "x").astype(bf16)
    gain_sum = exchange(gain_sum, "y", 1)
    near_part, far_part, gain_sum, grad_out = barrier((near_part, far_part, gain_sum, grad_out))
    near_total = scatter_direct(near_part, "zl")
    far_total = scatter_direct(far_part, "zl")
    gain_sum = exchange(gain_sum, "y", 2)

    next_down, back_down = finish(
        down_act[0], down_stash[0], down_grad[0], near_scale, near_total, gain_row
    )
    next_up, back_up = finish(far[0], far[1], far[2], far_scale, far_total, gain_row)

    next_down, back_down, next_up, back_up, gain_sum = barrier(
        (next_down, back_down, next_up, back_up, gain_sum)
    )
    gain_sum = exchange(gain_sum, "zl", 1)
    down_next = lax.ppermute(next_down, SEC, [(i, i + 1) for i in range(segments - 1)])
    down_back = lax.ppermute(back_down, SEC, [(i, i - 1) for i in range(1, segments)])
    up_next = lax.ppermute(next_up, SEC, [(i, segments - 2 - i) for i in range(segments - 1)])
    up_back = lax.ppermute(back_up, SEC, [(i, segments - i) for i in range(1, segments)])
    return (
        down_next[None],
        down_back[None],
        up_next[None],
        up_back[None],
        grad_in[None],
        grad_out[None],
        gain_sum[None],
    )


def solution(mesh):
    fine = Mesh(mesh.devices.reshape(4, 2, 4, 2, 4), AXES)
    tokens = P(SEC, TP, None)
    return jax.shard_map(
        body,
        mesh=fine,
        in_specs=(tokens,) * 6 + (P(SEC, None, TP), P(SEC, TP, None), P(SEC, None)),
        out_specs=(tokens,) * 4 + (P(SEC, None, TP), P(SEC, TP, None), P(SEC, None)),
        check_vma=False,
    )
```

```python
import jax
import jax.numpy as jnp
from jax.experimental import pallas as pl
from jax.experimental.pallas import tpu as pltpu
from jax import lax
from jax.sharding import Mesh
from jax.sharding import PartitionSpec as P

epsilon = 1e-05
root_coef = 0.7978845608028654
cubic_coef = 0.044715

f32 = jnp.float32
bf16 = jnp.bfloat16

AXES = ("zh", "core", "y", "zl", "x")
SIZES = {"x": 4, "y": 4, "zl": 2}
SEC = ("zh", "core")
TP = ("y", "zl", "x")


def shift(value, axis, k):
    n = SIZES[axis]
    return lax.ppermute(value, axis, [(i, (i + k) % n) for i in range(n)])


def gelu_both(preact):
    tanh_val = jnp.tanh(root_coef * (preact + cubic_coef * preact * preact * preact))
    value = 0.5 * preact * (1.0 + tanh_val)
    slope = 0.5 * (1.0 + tanh_val) + 0.5 * preact * (1.0 - tanh_val * tanh_val) * root_coef * (
        1.0 + 3.0 * cubic_coef * preact * preact
    )
    return value, slope


def row_scale_of(activ):
    widened = activ.astype(f32)
    return lax.rsqrt(jnp.mean(widened * widened, axis=-1, keepdims=True) + epsilon)


def contract_last(left, right):
    return lax.dot_general(left, right, (((1,), (1,)), ((), ())), preferred_element_type=f32)


def contract_first(left, right):
    return lax.dot_general(left, right, (((0,), (0,)), ((), ())), preferred_element_type=f32)


def scatter_direct(part, axis):
    m = part.shape[1] // SIZES[axis]
    total = part[:, :m].astype(f32)
    for k in range(1, SIZES[axis]):
        total = total + shift(part[:, k * m : (k + 1) * m], axis, k).astype(f32)
    return total


def added(left, right):
    return (left.astype(f32) + right.astype(f32)).astype(bf16)


def ring(block, axis):
    return shift(block, axis, -1), shift(block, axis, 1)


def ring_far(ahead, behind, axis):
    half = ahead.shape[1] // 2
    return shift(ahead[:, :half], axis, -1), shift(behind[:, half:], axis, 1)


def send_far(part, axis):
    half = part.shape[1] // 2
    return shift(part[:, :half], axis, 1), shift(part[:, half:], axis, -1)


def hand_over(part, low, high, axis):
    m = part.shape[1] // 3
    half = m // 2
    to_next = jnp.concatenate([added(part[:, m : m + half], low), part[:, m + half : 2 * m]], axis=1)
    to_last = jnp.concatenate([part[:, 2 * m : 2 * m + half], added(part[:, 2 * m + half :], high)], axis=1)
    return shift(to_next, axis, 1), shift(to_last, axis, -1)


def own_sum(part, from_last, from_next):
    m = part.shape[1] // 3
    return (part[:, :m].astype(f32) + from_last.astype(f32) + from_next.astype(f32)).astype(bf16)


def joined(block, ahead, low, high, behind):
    return jnp.concatenate([block, ahead, low, high, behind], axis=1)


def exchange(value, axis, bit):
    return value + lax.ppermute(value, axis, [(i, i ^ bit) for i in range(SIZES[axis])])


def weight_grad_kernel(*refs):
    normed, cot, slope_grad, hidden = [[r[...] for r in refs[2 * i : 2 * i + 2]] for i in range(4)]
    weight_ref, grad_in_ref, grad_out_ref, gain_ref = refs[8:]
    grad_out = contract_first(hidden[0], cot[0]) + contract_first(hidden[1], cot[1])
    grad_out_ref[...] = grad_out.astype(bf16)
    grad = contract_first(normed[0], slope_grad[0]) + contract_first(normed[1], slope_grad[1])
    grad_in_ref[...] = grad.astype(bf16)
    product = grad * weight_ref[...].astype(f32)
    high = product.astype(bf16)
    low = (product - high.astype(f32)).astype(bf16)
    ones = jnp.ones((8, grad.shape[1]), bf16)
    gain_ref[...] = contract_last(ones, high) + contract_last(ones, low)


def weight_grads(normed, cot, slope_grad, hidden, weight_in):
    width, units = weight_in.shape
    tile = 512
    wide = [pl.BlockSpec((v.shape[0], tile), lambda i: (0, i)) for v in (*normed, *cot)]
    whole = [pl.BlockSpec(v.shape, lambda i: (0, 0)) for v in (*slope_grad, *hidden)]
    tokens = sum(v.shape[0] for v in normed)
    return pl.pallas_call(
        weight_grad_kernel,
        grid=(width // tile,),
        in_specs=wide + whole + [pl.BlockSpec((tile, units), lambda i: (i, 0))],
        out_specs=[
            pl.BlockSpec((tile, units), lambda i: (i, 0)),
            pl.BlockSpec((units, tile), lambda i: (0, i)),
            pl.BlockSpec((8, tile), lambda i: (0, i)),
        ],
        out_shape=[
            jax.ShapeDtypeStruct((width, units), bf16),
            jax.ShapeDtypeStruct((units, width), bf16),
            jax.ShapeDtypeStruct((8, width), f32),
        ],
        compiler_params=pltpu.CompilerParams(vmem_limit_bytes=20 * 2**20),
        cost_estimate=pl.CostEstimate(
            flops=4 * tokens * width * units,
            bytes_accessed=2 * (2 * tokens * width + 3 * width * units),
            transcendentals=0,
        ),
    )(*normed, *cot, *slope_grad, *hidden, weight_in)


def products_kernel(
    acts_ref, normed_ref, cot_ref, weight_in_ref, weight_out_ref, part_ref, slope_ref, hidden_ref
):
    width = acts_ref.shape[1]
    step = 512

    def summed_in(left_ref):
        total = 0.0
        for at in range(0, width, step):
            total = total + jnp.dot(
                left_ref[:, at : at + step], weight_in_ref[at : at + step, :], preferred_element_type=f32
            )
        return total

    ahead = gelu_both(summed_in(acts_ref))[0].astype(bf16)
    value, slope = gelu_both(summed_in(normed_ref))
    back = 0.0
    for at in range(0, width, step):
        back = back + contract_last(cot_ref[:, at : at + step], weight_out_ref[:, at : at + step])
    slope_grad = (back * slope).astype(bf16)
    hidden_ref[...] = value.astype(bf16)
    slope_ref[...] = slope_grad
    for at in range(0, width, step):
        part_ref[0, :, at : at + step] = jnp.dot(
            ahead, weight_out_ref[:, at : at + step], preferred_element_type=f32
        ).astype(bf16)
        part_ref[1, :, at : at + step] = contract_last(
            slope_grad, weight_in_ref[at : at + step, :]
        ).astype(bf16)


def products_at_once(pieces, weight_in, weight_out):
    acts, normed, cot = [jnp.concatenate([p[k] for p in pieces]) for k in range(3)]
    tokens, width = acts.shape
    units = weight_in.shape[1]
    part, slope_grad, hidden = pl.pallas_call(
        products_kernel,
        in_specs=[pl.BlockSpec(memory_space=pltpu.VMEM)] * 5,
        out_specs=[pl.BlockSpec(memory_space=pltpu.VMEM)] * 3,
        out_shape=[
            jax.ShapeDtypeStruct((2, tokens, width), bf16),
            jax.ShapeDtypeStruct((tokens, units), bf16),
            jax.ShapeDtypeStruct((tokens, units), bf16),
        ],
        compiler_params=pltpu.CompilerParams(vmem_limit_bytes=40 * 2**20),
        cost_estimate=pl.CostEstimate(flops=1000, bytes_accessed=1000, transcendentals=0),
    )(acts, normed, cot, weight_in, weight_out)
    return part, (normed, cot, slope_grad, hidden)


def products(pieces, weight_in, weight_out):
    acts, normed, cot = [jnp.concatenate([p[k] for p in pieces]) for k in range(3)]
    hidden_ahead, _ = gelu_both(jnp.dot(acts, weight_in, preferred_element_type=f32))
    hidden_ahead = barrier(hidden_ahead.astype(bf16))
    summed = jnp.dot(hidden_ahead, weight_out, preferred_element_type=f32).astype(bf16)
    value, slope = gelu_both(jnp.dot(normed, weight_in, preferred_element_type=f32))
    slope_grad = (contract_last(cot, weight_out) * slope).astype(bf16)
    dnorm = contract_last(slope_grad, weight_in).astype(bf16)
    return jnp.stack([summed, dnorm]), (normed, cot, slope_grad, value.astype(bf16))


barrier = lax.optimization_barrier


def finish(act, stash, grad, scale, total, gain_row):
    ahead = (act.astype(f32) + total[0]).astype(bf16)
    widened = stash.astype(f32)
    weighted = total[1] * gain_row
    mixed_term = jnp.mean(weighted * widened, axis=-1, keepdims=True)
    back = (
        grad.astype(f32) + scale * weighted - widened * scale * scale * scale * mixed_term
    ).astype(bf16)
    return ahead, back


def prepare(act, stash, grad, gain_row):
    scale = row_scale_of(stash)
    act_normed = (act.astype(f32) * row_scale_of(act) * gain_row).astype(bf16)
    stash_normed = (stash.astype(f32) * scale * gain_row).astype(bf16)
    return jnp.stack([act_normed, stash_normed, grad]), scale


def body(down_act, down_stash, down_grad, up_act, up_stash, up_grad, w_in, w_out, norm_gain):
    weight_in = w_in[0]
    weight_out = w_out[0]
    gain_row = norm_gain[0]
    segments = 8
    mirror = [(i, segments - 1 - i) for i in range(segments)]
    incoming = jnp.stack([up_act[0], up_stash[0], up_grad[0]])
    far = lax.ppermute(incoming, SEC, mirror)
    near_block, near_scale = prepare(down_act[0], down_stash[0], down_grad[0], gain_row)
    near = jnp.concatenate([near_block, shift(near_block, "zl", 1)], axis=1)
    far, far_gain = barrier((far, gain_row))
    far_block, far_scale = prepare(far[0], far[1], far[2], far_gain)
    away = jnp.concatenate([far_block, shift(far_block, "zl", 1)], axis=1)

    near, away = barrier((near, away))
    na, nb = ring(near, "y")
    fa, fb = ring(away, "x")
    near = joined(near, na, *ring_far(na, nb, "y"), nb)
    away = joined(away, fa, *ring_far(fa, fb, "x"), fb)
    near, away = barrier((near, away))
    na, nb = ring(near, "x")
    fa, fb = ring(away, "y")
    nl, nh = ring_far(na, nb, "x")
    fl, fh = ring_far(fa, fb, "y")
    most, most_kept = products_at_once((near, na, nb, away, fa, fb), weight_in, weight_out)
    nl, nh, fl, fh, most, most_kept = barrier((nl, nh, fl, fh, most, most_kept))
    last, last_kept = products((nl, nh, fl, fh), weight_in, weight_out)

    rows = most.shape[1] // 2
    near_part, far_part = most[:, :rows], most[:, rows:]
    rows = last.shape[1] // 2
    nl, nh = send_far(last[:, :rows], "x")
    fl, fh = send_far(last[:, rows:], "y")
    nl, nh, fl, fh, most_kept, last_kept = barrier((nl, nh, fl, fh, most_kept, last_kept))
    n1, n3 = hand_over(near_part, nl, nh, "x")
    f1, f3 = hand_over(far_part, fl, fh, "y")
    grad_in, grad_out, gain_rows = weight_grads(*zip(most_kept, last_kept), weight_in)
    gain_sum = gain_rows[0] / gain_row
    gain_sum = exchange(exchange(gain_sum, "x", 1), "x", 2)
    n1, n3, f1, f3, gain_sum = barrier((n1, n3, f1, f3, gain_sum))

    near_part, far_part = own_sum(near_part, n1, n3), own_sum(far_part, f1, f3)
    near_part = scatter_direct(near_part, "y").astype(bf16)
    far_part = scatter_direct(far_part, "x").astype(bf16)
    gain_sum = exchange(gain_sum, "y", 1)
    near_part, far_part, gain_sum = barrier((near_part, far_part, gain_sum))
    near_total = scatter_direct(near_part, "zl")
    far_total = scatter_direct(far_part, "zl")
    gain_sum = exchange(gain_sum, "y", 2)

    next_down, back_down = finish(
        down_act[0], down_stash[0], down_grad[0], near_scale, near_total, gain_row
    )
    next_up, back_up = finish(far[0], far[1], far[2], far_scale, far_total, gain_row)

    next_down, back_down, next_up, back_up, gain_sum = barrier(
        (next_down, back_down, next_up, back_up, gain_sum)
    )
    gain_sum = exchange(gain_sum, "zl", 1)
    down_next = lax.ppermute(next_down, SEC, [(i, i + 1) for i in range(segments - 1)])
    down_back = lax.ppermute(back_down, SEC, [(i, i - 1) for i in range(1, segments)])
    up_next = lax.ppermute(next_up, SEC, [(i, segments - 2 - i) for i in range(segments - 1)])
    up_back = lax.ppermute(back_up, SEC, [(i, segments - i) for i in range(1, segments)])
    return (
        down_next[None],
        down_back[None],
        up_next[None],
        up_back[None],
        grad_in[None],
        grad_out[None],
        gain_sum[None],
    )


def solution(mesh):
    fine = Mesh(mesh.devices.reshape(4, 2, 4, 2, 4), AXES)
    tokens = P(SEC, TP, None)
    return jax.shard_map(
        body,
        mesh=fine,
        in_specs=(tokens,) * 6 + (P(SEC, None, TP), P(SEC, TP, None), P(SEC, None)),
        out_specs=(tokens,) * 4 + (P(SEC, None, TP), P(SEC, TP, None), P(SEC, None)),
        check_vma=False,
    )
```

```python
import jax
import jax.numpy as jnp
from jax.experimental import pallas as pl
from jax.experimental.pallas import tpu as pltpu
from jax import lax
from jax.sharding import Mesh
from jax.sharding import PartitionSpec as P

epsilon = 1e-05
root_coef = 0.7978845608028654
cubic_coef = 0.044715

f32 = jnp.float32
bf16 = jnp.bfloat16

AXES = ("zh", "core", "y", "zl", "x")
SIZES = {"x": 4, "y": 4, "zl": 2}
SEC = ("zh", "core")
TP = ("y", "zl", "x")


def shift(value, axis, k):
    n = SIZES[axis]
    return lax.ppermute(value, axis, [(i, (i + k) % n) for i in range(n)])


def gelu_both(preact):
    tanh_val = jnp.tanh(root_coef * (preact + cubic_coef * preact * preact * preact))
    value = 0.5 * preact * (1.0 + tanh_val)
    slope = 0.5 * (1.0 + tanh_val) + 0.5 * preact * (1.0 - tanh_val * tanh_val) * root_coef * (
        1.0 + 3.0 * cubic_coef * preact * preact
    )
    return value, slope


def row_scale_of(activ):
    widened = activ.astype(f32)
    return lax.rsqrt(jnp.mean(widened * widened, axis=-1, keepdims=True) + epsilon)


def contract_last(left, right):
    return lax.dot_general(left, right, (((1,), (1,)), ((), ())), preferred_element_type=f32)


def contract_first(left, right):
    return lax.dot_general(left, right, (((0,), (0,)), ((), ())), preferred_element_type=f32)


def scatter_direct(part, axis):
    m = part.shape[1] // SIZES[axis]
    total = part[:, :m].astype(f32)
    for k in range(1, SIZES[axis]):
        total = total + shift(part[:, k * m : (k + 1) * m], axis, k).astype(f32)
    return total


def added(left, right):
    return (left.astype(f32) + right.astype(f32)).astype(bf16)


def ring(block, axis):
    return shift(block, axis, -1), shift(block, axis, 1)


def ring_far(ahead, behind, axis):
    half = ahead.shape[1] // 2
    return shift(ahead[:, :half], axis, -1), shift(behind[:, half:], axis, 1)


def send_far(part, axis):
    half = part.shape[1] // 2
    return shift(part[:, :half], axis, 1), shift(part[:, half:], axis, -1)


def hand_over(part, low, high, axis):
    m = part.shape[1] // 3
    half = m // 2
    to_next = jnp.concatenate([added(part[:, m : m + half], low), part[:, m + half : 2 * m]], axis=1)
    to_last = jnp.concatenate([part[:, 2 * m : 2 * m + half], added(part[:, 2 * m + half :], high)], axis=1)
    return shift(to_next, axis, 1), shift(to_last, axis, -1)


def own_sum(part, from_last, from_next):
    m = part.shape[1] // 3
    return (part[:, :m].astype(f32) + from_last.astype(f32) + from_next.astype(f32)).astype(bf16)


def joined(block, ahead, low, high, behind):
    return jnp.concatenate([block, ahead, low, high, behind], axis=1)


def exchange(value, axis, bit):
    return value + lax.ppermute(value, axis, [(i, i ^ bit) for i in range(SIZES[axis])])


def weight_grad_kernel(*refs):
    normed, cot, slope_grad, hidden = [[r[...] for r in refs[2 * i : 2 * i + 2]] for i in range(4)]
    weight_ref, grad_in_ref, grad_out_ref, gain_ref = refs[8:]
    grad_out = contract_first(hidden[0], cot[0]) + contract_first(hidden[1], cot[1])
    grad_out_ref[...] = grad_out.astype(bf16)
    grad = contract_first(normed[0], slope_grad[0]) + contract_first(normed[1], slope_grad[1])
    grad_in_ref[...] = grad.astype(bf16)
    product = grad * weight_ref[...].astype(f32)
    high = product.astype(bf16)
    low = (product - high.astype(f32)).astype(bf16)
    ones = jnp.ones((8, grad.shape[1]), bf16)
    gain_ref[...] = contract_last(ones, high) + contract_last(ones, low)


def weight_grads(normed, cot, slope_grad, hidden, weight_in):
    width, units = weight_in.shape
    tile = 512
    wide = [pl.BlockSpec((v.shape[0], tile), lambda i: (0, i)) for v in (*normed, *cot)]
    whole = [pl.BlockSpec(v.shape, lambda i: (0, 0)) for v in (*slope_grad, *hidden)]
    tokens = sum(v.shape[0] for v in normed)
    return pl.pallas_call(
        weight_grad_kernel,
        grid=(width // tile,),
        in_specs=wide + whole + [pl.BlockSpec((tile, units), lambda i: (i, 0))],
        out_specs=[
            pl.BlockSpec((tile, units), lambda i: (i, 0)),
            pl.BlockSpec((units, tile), lambda i: (0, i)),
            pl.BlockSpec((8, tile), lambda i: (0, i)),
        ],
        out_shape=[
            jax.ShapeDtypeStruct((width, units), bf16),
            jax.ShapeDtypeStruct((units, width), bf16),
            jax.ShapeDtypeStruct((8, width), f32),
        ],
        compiler_params=pltpu.CompilerParams(vmem_limit_bytes=20 * 2**20),
        cost_estimate=pl.CostEstimate(
            flops=4 * tokens * width * units,
            bytes_accessed=2 * (2 * tokens * width + 3 * width * units),
            transcendentals=0,
        ),
    )(*normed, *cot, *slope_grad, *hidden, weight_in)


def products_kernel(
    acts_ref, normed_ref, cot_ref, weight_in_ref, weight_out_ref, part_ref, slope_ref, hidden_ref
):
    width = acts_ref.shape[1]
    step = 512

    def summed_in(left_ref):
        total = 0.0
        for at in range(0, width, step):
            total = total + jnp.dot(
                left_ref[:, at : at + step], weight_in_ref[at : at + step, :], preferred_element_type=f32
            )
        return total

    ahead = gelu_both(summed_in(acts_ref))[0].astype(bf16)
    value, slope = gelu_both(summed_in(normed_ref))
    back = 0.0
    for at in range(0, width, step):
        back = back + contract_last(cot_ref[:, at : at + step], weight_out_ref[:, at : at + step])
    slope_grad = (back * slope).astype(bf16)
    hidden_ref[...] = value.astype(bf16)
    slope_ref[...] = slope_grad
    for at in range(0, width, step):
        part_ref[0, :, at : at + step] = jnp.dot(
            ahead, weight_out_ref[:, at : at + step], preferred_element_type=f32
        ).astype(bf16)
        part_ref[1, :, at : at + step] = contract_last(
            slope_grad, weight_in_ref[at : at + step, :]
        ).astype(bf16)


def products_at_once(pieces, weight_in, weight_out):
    acts, normed, cot = [jnp.concatenate([p[k] for p in pieces]) for k in range(3)]
    tokens, width = acts.shape
    units = weight_in.shape[1]
    part, slope_grad, hidden = pl.pallas_call(
        products_kernel,
        in_specs=[pl.BlockSpec(memory_space=pltpu.VMEM)] * 5,
        out_specs=[pl.BlockSpec(memory_space=pltpu.VMEM)] * 3,
        out_shape=[
            jax.ShapeDtypeStruct((2, tokens, width), bf16),
            jax.ShapeDtypeStruct((tokens, units), bf16),
            jax.ShapeDtypeStruct((tokens, units), bf16),
        ],
        compiler_params=pltpu.CompilerParams(vmem_limit_bytes=40 * 2**20),
        cost_estimate=pl.CostEstimate(flops=1000, bytes_accessed=1000, transcendentals=0),
    )(acts, normed, cot, weight_in, weight_out)
    return part, (normed, cot, slope_grad, hidden)


def products(pieces, weight_in, weight_out):
    acts, normed, cot = [jnp.concatenate([p[k] for p in pieces]) for k in range(3)]
    hidden_ahead, _ = gelu_both(jnp.dot(acts, weight_in, preferred_element_type=f32))
    hidden_ahead = barrier(hidden_ahead.astype(bf16))
    summed = jnp.dot(hidden_ahead, weight_out, preferred_element_type=f32).astype(bf16)
    value, slope = gelu_both(jnp.dot(normed, weight_in, preferred_element_type=f32))
    slope_grad = (contract_last(cot, weight_out) * slope).astype(bf16)
    dnorm = contract_last(slope_grad, weight_in).astype(bf16)
    return jnp.stack([summed, dnorm]), (normed, cot, slope_grad, value.astype(bf16))


barrier = lax.optimization_barrier


def finish(act, stash, grad, scale, total, gain_row):
    ahead = (act.astype(f32) + total[0]).astype(bf16)
    widened = stash.astype(f32)
    weighted = total[1] * gain_row
    mixed_term = jnp.mean(weighted * widened, axis=-1, keepdims=True)
    back = (
        grad.astype(f32) + scale * weighted - widened * scale * scale * scale * mixed_term
    ).astype(bf16)
    return ahead, back


def prepare(act, stash, grad, gain_row):
    scale = row_scale_of(stash)
    act_normed = (act.astype(f32) * row_scale_of(act) * gain_row).astype(bf16)
    stash_normed = (stash.astype(f32) * scale * gain_row).astype(bf16)
    return jnp.stack([act_normed, stash_normed, grad]), scale


def body(down_act, down_stash, down_grad, up_act, up_stash, up_grad, w_in, w_out, norm_gain):
    weight_in = w_in[0]
    weight_out = w_out[0]
    gain_row = norm_gain[0]
    segments = 8
    mirror = [(i, segments - 1 - i) for i in range(segments)]
    incoming = jnp.stack([up_act[0], up_stash[0], up_grad[0]])
    far = lax.ppermute(incoming, SEC, mirror)
    near_block, near_scale = prepare(down_act[0], down_stash[0], down_grad[0], gain_row)
    near = jnp.concatenate([near_block, shift(near_block, "zl", 1)], axis=1)
    far, far_gain = barrier((far, gain_row))
    far_block, far_scale = prepare(far[0], far[1], far[2], far_gain)
    away = jnp.concatenate([far_block, shift(far_block, "zl", 1)], axis=1)

    near, away = barrier((near, away))
    na, nb = ring(near, "y")
    fa, fb = ring(away, "x")
    near = joined(near, na, *ring_far(na, nb, "y"), nb)
    away = joined(away, fa, *ring_far(fa, fb, "x"), fb)
    near, away = barrier((near, away))
    na, nb = ring(near, "x")
    fa, fb = ring(away, "y")
    nl, nh = ring_far(na, nb, "x")
    fl, fh = ring_far(fa, fb, "y")
    most, most_kept = products_at_once((near, na, nb, away, fa, fb), weight_in, weight_out)
    nl, nh, fl, fh, most, most_kept = barrier((nl, nh, fl, fh, most, most_kept))
    last, last_kept = products((nl, nh, fl, fh), weight_in, weight_out)

    rows = most.shape[1] // 2
    near_part, far_part = most[:, :rows], most[:, rows:]
    rows = last.shape[1] // 2
    nl, nh = send_far(last[:, :rows], "x")
    fl, fh = send_far(last[:, rows:], "y")
    nl, nh, fl, fh, most_kept, last_kept = barrier((nl, nh, fl, fh, most_kept, last_kept))
    n1, n3 = hand_over(near_part, nl, nh, "x")
    f1, f3 = hand_over(far_part, fl, fh, "y")
    grad_in, grad_out, gain_rows = weight_grads(*zip(most_kept, last_kept), weight_in)
    gain_sum = gain_rows[0] / gain_row
    gain_sum = exchange(exchange(gain_sum, "x", 1), "x", 2)
    n1, n3, f1, f3, gain_sum = barrier((n1, n3, f1, f3, gain_sum))

    near_part, far_part = own_sum(near_part, n1, n3), own_sum(far_part, f1, f3)
    near_part = scatter_direct(near_part, "y").astype(bf16)
    far_part = scatter_direct(far_part, "x").astype(bf16)
    gain_sum = exchange(gain_sum, "y", 1)
    near_part, far_part, gain_sum = barrier((near_part, far_part, gain_sum))
    totals = scatter_direct(jnp.concatenate([near_part, far_part]), "zl")
    near_total, far_total = totals[:2], totals[2:]
    gain_sum = exchange(gain_sum, "y", 2)

    next_down, back_down = finish(
        down_act[0], down_stash[0], down_grad[0], near_scale, near_total, gain_row
    )
    next_up, back_up = finish(far[0], far[1], far[2], far_scale, far_total, gain_row)

    next_down, back_down, next_up, back_up, gain_sum = barrier(
        (next_down, back_down, next_up, back_up, gain_sum)
    )
    gain_sum = exchange(gain_sum, "zl", 1)
    down_next = lax.ppermute(next_down, SEC, [(i, i + 1) for i in range(segments - 1)])
    down_back = lax.ppermute(back_down, SEC, [(i, i - 1) for i in range(1, segments)])
    up_next = lax.ppermute(next_up, SEC, [(i, segments - 2 - i) for i in range(segments - 1)])
    up_back = lax.ppermute(back_up, SEC, [(i, segments - i) for i in range(1, segments)])
    return (
        down_next[None],
        down_back[None],
        up_next[None],
        up_back[None],
        grad_in[None],
        grad_out[None],
        gain_sum[None],
    )


def solution(mesh):
    fine = Mesh(mesh.devices.reshape(4, 2, 4, 2, 4), AXES)
    tokens = P(SEC, TP, None)
    return jax.shard_map(
        body,
        mesh=fine,
        in_specs=(tokens,) * 6 + (P(SEC, None, TP), P(SEC, TP, None), P(SEC, None)),
        out_specs=(tokens,) * 4 + (P(SEC, None, TP), P(SEC, TP, None), P(SEC, None)),
        check_vma=False,
    )
```
